256 devices in a mesh: dp: 16 (over z_lo, y, core), tensor: 16 (over x, z_hi).
Axes of the slice: x: 4, y: 4, z: 8 (z_hi: 4, z_lo: 2; z = z_hi * 2 + z_lo), core: 2. Of those that a mesh axis runs over, the one named last changes fastest.
Arguments:
- layer_input: bfloat16 [8192, 6144], P(('dp', 'tensor')), may hold values from -24 to 24
- out_grad: bfloat16 [8192, 6144], P('dp', 'tensor'), may hold values from -6 to 6
- master: float32 [6144, 6144], P('dp', 'tensor'), may hold values from -300 to 300
- moment_code: bfloat16 [6144, 6144], P('dp', 'tensor'), may hold values from -1 to 1
- moment_scale: float32 [6144, 48], P('dp', 'tensor'), may hold values from 0.1 to 3
- second_code: bfloat16 [6144, 6144], P('dp', 'tensor'), may hold values from 0.049804688 to 1
- second_scale: float32 [6144, 48], P('dp', 'tensor'), may hold values from 0.001 to 0.01
Outputs:
- input_grad: bfloat16 [8192, 6144], P(('dp', 'tensor'))
- new_master: float32 [6144, 6144], P('dp', 'tensor')
- new_moment_code: bfloat16 [6144, 6144], P('dp', 'tensor')
- new_moment_scale: float32 [6144, 48], P('dp', 'tensor')
- new_second_code: bfloat16 [6144, 6144], P('dp', 'tensor')
- new_second_scale: float32 [6144, 48], P('dp', 'tensor')
- new_weight: bfloat16 [6144, 6144], P(None, 'tensor')
- trust_ratio: float32 [], replicated
The draws below stay inside these ranges and needn't reach their ends.
All inputs are finite; a program needn't handle non-finite values. Where the reference program divides by a largest or mean magnitude, that divisor is 1e-20 or more.
Results may differ from the reference program's by a relative error of at most 0.017.
Values may be sent and summed in bfloat16 or wider, within the bound.
No kernel may reach another device: no remote copies, remote signals or barrier semaphores. Data moves between devices by JAX's collectives and lax.ppermute only.
A program may use at most 128 MiB of HBM per device.

```python
import math
import jax
import jax.numpy as jnp
from jax import lax

FEAT_IN = 6144
FEAT_OUT = 6144
QBLOCK = 128
TOKENS = 8192
N_TENSOR = 16


def draw_master(key, part):
    key = jax.random.fold_in(key, 11)
    first, second, third = jax.random.split(key, 3)
    row_pos = jnp.arange(FEAT_IN, dtype=jnp.float32) / max(FEAT_IN - 1, 1)
    col_pos = jnp.arange(FEAT_OUT, dtype=jnp.float32) / max(FEAT_OUT - 1, 1)
    ramp = jnp.exp(0.5 * math.log(3.0) * (row_pos[:, None] + col_pos[None, :]))
    row_scale = jnp.exp(0.5 * math.log(10.0) * jax.random.uniform(second, (FEAT_IN,), jnp.float32))
    col_scale = jnp.exp(0.5 * math.log(10.0) * jax.random.uniform(third, (FEAT_OUT,), jnp.float32))
    base = jnp.clip(jax.random.normal(first, (FEAT_IN, FEAT_OUT), jnp.float32), -6.0, 6.0)
    return (0.25 * base * row_scale[:, None] * col_scale[None, :] * ramp).astype(jnp.float32)


def draw_moment_scale(key, part):
    key = jax.random.fold_in(key, 23)
    blocks = FEAT_OUT // QBLOCK
    row_pos = jnp.arange(FEAT_IN, dtype=jnp.float32) / max(FEAT_IN - 1, 1)
    col_pos = jnp.arange(blocks, dtype=jnp.float32) / max(blocks - 1, 1)
    ramp = jnp.exp(0.5 * math.log(3.0) * (2.0 - row_pos[:, None] - col_pos[None, :]))
    spread = jnp.exp(math.log(10.0) * jax.random.uniform(key, (FEAT_IN, blocks), jnp.float32))
    return (0.1 * spread * ramp).astype(jnp.float32)


def with_spikes(result, key, source, target, shards_of, factor):
    owner, partner = [(jnp.arange(result.shape[axis_at]) // (result.shape[axis_at] // shards_of)).reshape([-1 if axis == axis_at else 1 for axis in range(result.ndim)]) for axis_at in (source, target)]
    chosen = jax.random.permutation(key, shards_of)[partner]
    strong = (owner == chosen) | (owner == (partner + shards_of // 2) % shards_of)
    return jnp.where(strong, factor * result, result)


def levels(rng, dims, pieces, smallest, largest):
    loudness = 1.0
    for axis_at, blocks in pieces:
        heights = jax.random.uniform(jax.random.fold_in(jax.random.fold_in(rng, 6), axis_at), (blocks,), jnp.float32, smallest / len(pieces), largest / len(pieces))
        loudness = loudness * jnp.repeat(jnp.exp(heights), dims[axis_at] // blocks).reshape((-1,) + (1,) * (len(dims) - 1 - axis_at))
    return loudness


def heavy_noise(rng, extent, scale, most, pieces, heavy, kind=jnp.bfloat16):
    drawn = scale * jax.random.normal(rng, extent, jnp.float32)
    if pieces:
        drawn = drawn * levels(rng, extent, pieces, -0.22, 0.18)
    return jnp.clip(with_spikes(drawn, jax.random.fold_in(rng, 3), *heavy), -most, most).astype(kind)


def setup_inputs(seed: int = 0) -> dict:
    streams_of = jax.random.split(jax.random.key(seed), 8)
    layer_input = heavy_noise(streams_of[0], (TOKENS, FEAT_IN), 1.0, 24.0, ((0, 256),), (0, 1, 256, 6.0))
    out_grad = heavy_noise(streams_of[1], (TOKENS, FEAT_OUT), 1.0, 6.0, ((0, 16), (1, 16)), (1, 0, 16, 2.0))
    master = draw_master(jax.random.fold_in(streams_of[7], 71), 0)
    moment_code = jnp.clip(jax.random.uniform(streams_of[3], (FEAT_IN, FEAT_OUT), jnp.float32, -1.0, 1.0) * levels(streams_of[3], (FEAT_IN, FEAT_OUT), ((0, 16), (1, 16)), -0.4, 0.0), -1.0, 1.0).astype(jnp.bfloat16)
    moment_scale = draw_moment_scale(jax.random.fold_in(streams_of[7], 71), 0)
    second_code = jnp.clip(0.049804688 + 0.9501953 * jax.random.uniform(streams_of[5], (FEAT_IN, FEAT_OUT), jnp.float32) ** levels(streams_of[5], (FEAT_IN, FEAT_OUT), ((0, 16), (1, 16)), -0.2, 0.2), 0.049804688, 1.0).astype(jnp.bfloat16)
    second_scale = jnp.clip(jnp.exp(math.log(0.01) - 2.30258502 * jax.random.uniform(streams_of[6], (FEAT_IN, FEAT_OUT // QBLOCK), jnp.float32) ** levels(streams_of[6], (FEAT_IN, FEAT_OUT // QBLOCK), ((0, 16), (1, 16)), -0.2, 0.2)), 0.001, 0.01)
    return dict(layer_input=layer_input, out_grad=out_grad, master=master, moment_code=moment_code, moment_scale=moment_scale, second_code=second_code, second_scale=second_scale)


def dequant(code, scale):
    rows, cols = code.shape
    blocks = scale.shape[1]
    shaped = code.astype(jnp.float32).reshape(rows, blocks, cols // blocks)
    return (shaped * scale[:, :, None]).reshape(rows, cols)

def requant(values, blocks):
    rows, cols = values.shape
    shaped = values.reshape(rows, blocks, cols // blocks)
    scale = 2.0 * lax.optimization_barrier(jnp.max(jnp.abs(shaped), axis=2)) + 1e-06
    code = (shaped / scale[:, :, None]).astype(jnp.bfloat16).reshape(rows, cols)
    return (code, scale)

def reference(layer_input, out_grad, master, moment_code, moment_scale, second_code, second_scale):
    inv_root = 1.0 / math.sqrt(FEAT_IN)
    weight16 = master.astype(jnp.bfloat16)
    width = FEAT_OUT // N_TENSOR
    grad_blocks = out_grad.reshape(TOKENS, N_TENSOR, width).transpose(1, 0, 2)
    weight_blocks = weight16.reshape(FEAT_IN, N_TENSOR, width).transpose(1, 0, 2)

    def add_block(total, pair):
        grad_part, weight_part = pair
        term = jnp.einsum('tn,kn->tk', grad_part, weight_part, preferred_element_type=jnp.float32) * inv_root
        term = lax.optimization_barrier(term.astype(jnp.bfloat16)).astype(jnp.float32)
        return (total + term, None)
    summed, _ = lax.scan(add_block, jnp.zeros((TOKENS, FEAT_IN), jnp.float32), (grad_blocks, weight_blocks))
    input_grad = summed.astype(jnp.bfloat16)
    grad = jnp.einsum('tk,tn->kn', layer_input, out_grad, preferred_element_type=jnp.float32) * inv_root
    moment = dequant(moment_code, moment_scale)
    second = dequant(second_code, second_scale)
    moment_next = 0.9 * moment + 0.1 * grad
    second_next = 0.999 * second + 0.001 * grad * grad
    update = moment_next / (1.0 - 0.9 ** 10) / (jnp.sqrt(second_next / (1.0 - 0.999 ** 10)) + 1e-06) + 0.1 * master
    weight_sq = jnp.sum(master * master)
    update_sq = jnp.sum(update * update)
    trust_ratio = jnp.sqrt(weight_sq) / (jnp.sqrt(update_sq) + 1e-06)
    new_master = master - 0.02 * trust_ratio * update
    blocks = moment_scale.shape[1]
    new_moment_code, new_moment_scale = requant(moment_next, blocks)
    new_second_code, new_second_scale = requant(second_next, blocks)
    new_weight = new_master.astype(jnp.bfloat16)
    return (input_grad, new_master, new_moment_code, new_moment_scale, new_second_code, new_second_scale, new_weight, trust_ratio)
```

```python
import math

import jax
import jax.numpy as jnp
from jax import lax
from jax.sharding import PartitionSpec as P

FEAT_IN = 6144
SIZES = (2, 4, 2, 4, 4)
BOTH = ("dp", "tensor")


def shift(array, z=0, y=0, core=0, x=0, high=0):
    moves = (z, y, core, x, high)
    pairs = []
    for source in range(math.prod(SIZES)):
        rest, place = source, []
        for size in reversed(SIZES):
            place.append(rest % size)
            rest //= size
        target = 0
        for size, at, move in zip(SIZES, reversed(place), moves):
            target = target * size + (at + move) % size
        pairs.append((source, target))
    return lax.ppermute(array, BOTH, pairs)


def roll(array, start):
    return lax.dynamic_slice_in_dim(
        jnp.concatenate([array, array], axis=0), start, array.shape[0], axis=0
    )


def at(array, index, axis):
    return lax.dynamic_index_in_dim(array, index, axis, keepdims=False)


def dequant(code, scale):
    rows, cols = code.shape
    blocks = scale.shape[1]
    shaped = code.astype(jnp.float32).reshape(rows, blocks, cols // blocks)
    return (shaped * scale[:, :, None]).reshape(rows, cols)


def requant(values, blocks):
    rows, cols = values.shape
    shaped = values.reshape(rows, blocks, cols // blocks)
    scale = 2.0 * jnp.max(jnp.abs(shaped), axis=2) + 1e-06
    code = (shaped / scale[:, :, None]).astype(jnp.bfloat16).reshape(rows, cols)
    return (code, scale)


def total_of(values):
    row = jnp.concatenate([jnp.full((1, 128), v, jnp.float32) for v in values] * (8 // len(values)))
    for axis in ("dp", "tensor"):
        spread = jnp.broadcast_to(row[None], (16, 8, 128))
        row = jnp.sum(lax.all_to_all(spread, axis, 0, 0, tiled=True), axis=0)
    return [row[i, 0] for i in range(len(values))]


def local(layer_input, out_grad, master, moment_code, moment_scale, second_code, second_scale):
    inv_root = 1.0 / math.sqrt(FEAT_IN)
    bf16, f32 = jnp.bfloat16, jnp.float32
    d, t = lax.axis_index("dp"), lax.axis_index("tensor")
    z, y, core, x, high = d // 8, (d // 2) % 4, d % 2, t // 4, t % 4
    few, feat = layer_input.shape
    rows, cols = master.shape
    pair = 2 * rows

    grads = out_grad.reshape(4, 4, few, cols)
    grads = roll(grads[::-1], 3 - x)
    parts = [at(grads, high, 1)] + [
        shift(at(grads, (high + s) % 4, 1), high=s) for s in (1, 2, 3)
    ]
    wide = jnp.concatenate(parts, axis=2)
    wide = jnp.stack([wide, shift(wide, z=1)])
    wide = jnp.stack([wide] + [shift(wide, y=s) for s in (1, 2, 3)])
    wide = wide.reshape(32 * few, 4 * cols)

    blocks = layer_input.reshape(few, 2, 4, pair)
    mine = [at(blocks, y, 2)] + [shift(at(blocks, (y + s) % 4, 2), y=s) for s in (1, 2, 3)]
    mine = jnp.stack(mine)
    mine = jnp.stack([at(mine, z, 2), shift(at(mine, 1 - z, 2), z=1)], axis=1)
    acts = jnp.stack([mine] + [shift(mine, x=s) for s in (1, 2, 3)], axis=2)
    acts = acts.reshape(32 * few, pair)

    part = (jnp.einsum("tk,tn->kn", acts, wide, preferred_element_type=f32) * inv_root).reshape(
        2, rows, 4 * cols
    )
    part = at(part, core, 0) + shift(at(part, 1 - core, 0).astype(bf16), core=1).astype(f32)
    part = part.reshape(rows, 4, cols)
    grad = part[:, 0]
    for s in (1, 2, 3):
        grad = grad + shift(part[:, s].astype(bf16), high=-s).astype(f32)

    weight16 = master.astype(bf16)
    weights = jnp.concatenate(
        [weight16] + [shift(weight16, high=s) for s in (1, 2, 3)], axis=1
    )
    other = shift(weights, core=1)
    weights = jnp.concatenate(
        [jnp.where(core == 0, weights, other), jnp.where(core == 0, other, weights)]
    )
    outs = (
        jnp.einsum("tn,kn->tk", wide, weights, preferred_element_type=f32) * inv_root
    ).reshape(4, 2, 4, few, pair)
    summed = outs[:, :, 0]
    for s in (1, 2, 3):
        summed = summed + shift(outs[:, :, s].astype(bf16), x=-s).astype(f32)
    summed = summed.astype(bf16)
    back = jnp.stack([summed[0]] + [shift(summed[s], y=-s) for s in (1, 2, 3)])
    near, far = back[:, 0], shift(back[:, 1], z=1)
    near, far = jnp.where(z == 0, near, far), jnp.where(z == 0, far, near)
    back = roll(jnp.stack([near, far], axis=1), (4 - y) % 4)
    input_grad = back.transpose(2, 1, 0, 3).reshape(few, feat)

    moment = dequant(moment_code, moment_scale)
    second = dequant(second_code, second_scale)
    moment_next = 0.9 * moment + 0.1 * grad
    second_next = 0.999 * second + 0.001 * grad * grad
    update = (
        moment_next / (1.0 - 0.9**10) / (jnp.sqrt(second_next / (1.0 - 0.999**10)) + 1e-06)
        + 0.1 * master
    )
    weight_sq, update_sq = total_of((jnp.sum(master * master), jnp.sum(update * update)))
    trust_ratio = jnp.sqrt(weight_sq) / (jnp.sqrt(update_sq) + 1e-06)
    new_master = master - 0.02 * trust_ratio * update
    blocks = moment_scale.shape[1]
    new_moment_code, new_moment_scale = requant(moment_next, blocks)
    new_second_code, new_second_scale = requant(second_next, blocks)

    new16 = new_master.astype(bf16)
    new16 = jnp.stack([new16, shift(new16, z=1)])
    out = jnp.zeros((2, 4, 2, rows, cols), bf16)
    for s in (0, 1, 2, 3):
        piece = new16 if s == 0 else shift(new16, y=s)
        twin = shift(piece, core=1)
        from_y = (y + 4 - s) % 4
        for c, both in ((core, piece), (1 - core, twin)):
            for r in (0, 1):
                out = lax.dynamic_update_slice(
                    out, both[r][None, None, None], ((z + r) % 2, from_y, c, 0, 0)
                )
    new_weight = out.reshape(16 * rows, cols)
    return (
        input_grad,
        new_master,
        new_moment_code,
        new_moment_scale,
        new_second_code,
        new_second_scale,
        new_weight,
        trust_ratio,
    )


def solution(mesh):
    placed = (P(BOTH, None),) + (P("dp", "tensor"),) * 6
    return jax.shard_map(
        local,
        mesh=mesh,
        in_specs=placed,
        out_specs=(P(BOTH, None),) + (P("dp", "tensor"),) * 5 + (P(None, "tensor"), P()),
        check_vma=False,
    )
```

```python
import functools
import math

import jax
import jax.numpy as jnp
from jax import lax
from jax.experimental import pallas as pl
from jax.experimental.pallas import tpu as pltpu
from jax.sharding import PartitionSpec as P

FEAT_IN = 6144
SIZES = (2, 4, 2, 4, 4)
BOTH = ("dp", "tensor")
BF16, F32 = jnp.bfloat16, jnp.float32


def shift(array, z=0, y=0, core=0, x=0, high=0):
    moves = (z, y, core, x, high)
    pairs = []
    for source in range(math.prod(SIZES)):
        rest, place = source, []
        for size in reversed(SIZES):
            place.append(rest % size)
            rest //= size
        target = 0
        for size, at, move in zip(SIZES, reversed(place), moves):
            target = target * size + (at + move) % size
        pairs.append((source, target))
    return lax.ppermute(array, BOTH, pairs)


def roll(array, start):
    return lax.dynamic_slice_in_dim(
        jnp.concatenate([array, array], axis=0), start, array.shape[0], axis=0
    )


def take(array, index, axis):
    return lax.dynamic_index_in_dim(array, index, axis, keepdims=False)


def after(array, *others):
    return lax.optimization_barrier((array,) + others)[0]


def total_of(values):
    row = jnp.concatenate([jnp.full((1, 128), v, F32) for v in values] * (8 // len(values)))
    for axis in ("dp", "tensor"):
        spread = jnp.broadcast_to(row[None], (16, 8, 128))
        row = jnp.sum(lax.all_to_all(spread, axis, 0, 0, tiled=True), axis=0)
    return [row[i, 0] for i in range(len(values))]


def moments_kernel(
    own, one, two, three, master, mcode, mscale, scode, sscale,
    update, new_mcode, new_mscale, new_scode, new_sscale, sums,
):
    rows, cols = master.shape
    blocks = mscale.shape[1]
    wide = cols // blocks
    step = 64
    sums[...] = jnp.zeros_like(sums)

    def body(i, carry):
        at = pl.ds(pl.multiple_of(i * step, step), step)
        mscales, sscales = mscale[at, :], sscale[at, :]
        new_m, new_s = [], []
        for b in range(blocks):
            cut = slice(b * wide, (b + 1) * wide)
            grad = (
                own[at, cut]
                + one[at, cut].astype(F32)
                + two[at, cut].astype(F32)
                + three[at, cut].astype(F32)
            )
            weight = master[at, cut]
            moment = mcode[at, cut].astype(F32) * mscales[:, b : b + 1]
            second = scode[at, cut].astype(F32) * sscales[:, b : b + 1]
            moment = 0.9 * moment + 0.1 * grad
            second = 0.999 * second + 0.001 * grad * grad
            change = (
                moment / (1.0 - 0.9**10) / (jnp.sqrt(second / (1.0 - 0.999**10)) + 1e-06)
                + 0.1 * weight
            )
            update[at, cut] = change
            mtop = 2.0 * jnp.max(jnp.abs(moment), axis=1, keepdims=True) + 1e-06
            stop = 2.0 * jnp.max(jnp.abs(second), axis=1, keepdims=True) + 1e-06
            new_mcode[at, cut] = (moment / mtop).astype(BF16)
            new_scode[at, cut] = (second / stop).astype(BF16)
            new_m.append(mtop)
            new_s.append(stop)
            sums[0:1, :] += jnp.sum(weight * weight, axis=0, keepdims=True)
            sums[1:2, :] += jnp.sum(change * change, axis=0, keepdims=True)
        new_mscale[at, :] = jnp.concatenate(new_m, axis=1)
        new_sscale[at, :] = jnp.concatenate(new_s, axis=1)
        return carry

    lax.fori_loop(0, rows // step, body, 0)


def moments(own, others, master, mcode, mscale, scode, sscale):
    like = lambda a, dtype: jax.ShapeDtypeStruct(a.shape, dtype)
    block = master.shape[1] // mscale.shape[1]
    return pl.pallas_call(
        moments_kernel,
        out_shape=(
            like(master, F32),
            like(master, BF16),
            like(mscale, F32),
            like(master, BF16),
            like(sscale, F32),
            jax.ShapeDtypeStruct((8, block), F32),
        ),
        in_specs=[pl.BlockSpec(memory_space=pltpu.VMEM)] * 9,
        out_specs=[pl.BlockSpec(memory_space=pltpu.VMEM)] * 6,
        compiler_params=pltpu.CompilerParams(vmem_limit_bytes=32 * 1024 * 1024),
        cost_estimate=pl.CostEstimate(
            flops=40 * master.size, bytes_accessed=24 * master.size, transcendentals=master.size
        ),
    )(own, *others, master, mcode, mscale, scode, sscale)


def gather_rows(part):
    far = shift(part, z=1)
    near = [part] + [shift(part, y=s) for s in (1, 2, 3)]
    far = [far] + [shift(far, y=s) for s in (1, 2, 3)]
    pieces = []
    for r, row in enumerate((near, far)):
        for s, piece in enumerate(row):
            pieces.append(((r, s, 0), piece))
            pieces.append(((r, s, 1), shift(piece, core=1)))
    return pieces


def place_kernel(count, order, *refs):
    pieces, out = refs[:count], refs[count]
    step = pl.program_id(0)
    for i in range(count):

        @pl.when(step == i)
        def _(i=i):
            out[...] = pieces[i][...]


def place_rows(pieces, z, y, core):
    count = len(pieces)
    rows, cols = pieces[0][1].shape
    order = jnp.stack(
        [
            ((z + r) % 2 * 4 + (y + 4 - s) % 4) * 2 + (core + c) % 2
            for (r, s, c), _ in pieces
        ]
    ).astype(jnp.int32)
    return pl.pallas_call(
        functools.partial(place_kernel, count),
        out_shape=jax.ShapeDtypeStruct((count * rows, cols), BF16),
        grid_spec=pltpu.PrefetchScalarGridSpec(
            num_scalar_prefetch=1,
            grid=(count,),
            in_specs=[pl.BlockSpec((rows, cols), lambda i, order: (0, 0))] * count,
            out_specs=pl.BlockSpec((rows, cols), lambda i, order: (order[i], 0)),
        ),
        compiler_params=pltpu.CompilerParams(vmem_limit_bytes=32 * 1024 * 1024),
        cost_estimate=pl.CostEstimate(
            flops=0, bytes_accessed=4 * count * rows * cols, transcendentals=0
        ),
    )(order, *[piece for _, piece in pieces])


def local(layer_input, out_grad, master, moment_code, moment_scale, second_code, second_scale):
    inv_root = 1.0 / math.sqrt(FEAT_IN)
    d, t = lax.axis_index("dp"), lax.axis_index("tensor")
    z, y, core, x, high = d // 8, (d // 2) % 4, d % 2, t // 4, t % 4
    few, feat = layer_input.shape
    rows, cols = master.shape
    steps = (1, 2, 3)

    grads = out_grad.reshape(4, 4, few, cols)
    grads = roll(grads[::-1], 3 - x)
    parts = [take(grads, high, 1)] + [
        shift(take(grads, (high + s) % 4, 1), high=s) for s in steps
    ]
    near = jnp.concatenate(parts, axis=2).reshape(4 * few, 4 * cols)
    far = shift(near, z=1)
    crossed = far
    near = jnp.concatenate([near] + [shift(near, y=s) for s in steps])
    far = jnp.concatenate([far] + [shift(far, y=s) for s in steps])
    wide = [near, shift(near, core=1), far, shift(far, core=1)]

    mine = layer_input.reshape(few, 2, 4, 2, rows)
    mine = jnp.stack([take(mine, core, 3), shift(take(mine, 1 - core, 3), core=1)])
    mine = jnp.stack(
        [take(mine, y, 3)] + [shift(take(mine, (y + s) % 4, 3), y=s) for s in steps], axis=1
    )
    mine = jnp.stack([take(mine, z, 3), shift(take(mine, 1 - z, 3), z=1)])
    acts = jnp.stack([mine] + [shift(mine, x=s) for s in steps], axis=3)
    acts = acts.reshape(4, 16 * few, rows)

    part = sum(
        jnp.einsum("tk,tn->kn", acts[i], wide[i], preferred_element_type=F32) for i in range(4)
    )
    part = (part * inv_root).reshape(rows, 4, cols)
    sends = [part[:, s].astype(BF16) for s in steps]
    others = [shift(send, high=-s) for s, send in zip(steps, sends)]

    update, new_moment_code, new_moment_scale, new_second_code, new_second_scale, sums = moments(
        part[:, 0], others, master, moment_code, moment_scale, second_code, second_scale
    )

    weight16 = after(master.astype(BF16), crossed)
    weights = jnp.concatenate([weight16] + [shift(weight16, high=s) for s in steps], axis=1)
    weights = after(weights, *sends)
    outs = jnp.stack(
        [jnp.einsum("tn,kn->tk", w, weights, preferred_element_type=F32) for w in wide]
    )
    outs = (outs * inv_root).reshape(2, 2, 4, 4, few, rows)
    summed = outs[:, :, :, 0]
    for s in steps:
        summed = summed + shift(outs[:, :, :, s].astype(BF16), x=-s).astype(F32)
    back = summed.astype(BF16)
    near, far = back[0], shift(back[1], z=1)
    back = jnp.stack([jnp.where(z == 0, near, far), jnp.where(z == 0, far, near)], axis=2)
    back = jnp.stack([back[:, 0]] + [shift(back[:, s], y=-s) for s in steps], axis=2)
    near, far = back[0], shift(back[1], core=1)
    back = jnp.stack([jnp.where(core == 0, near, far), jnp.where(core == 0, far, near)])
    back = roll(back.transpose(2, 0, 1, 3, 4), (4 - y) % 4)
    input_grad = back.transpose(3, 2, 0, 1, 4).reshape(few, feat)

    weight_sq, update_sq = total_of((jnp.sum(sums[0]), jnp.sum(sums[1])))
    trust_ratio = jnp.sqrt(weight_sq) / (jnp.sqrt(update_sq) + 1e-06)
    new_master = master - 0.02 * trust_ratio * update
    new_weight = place_rows(gather_rows(new_master.astype(BF16)), z, y, core)
    return (
        input_grad,
        new_master,
        new_moment_code,
        new_moment_scale,
        new_second_code,
        new_second_scale,
        new_weight,
        trust_ratio,
    )


def solution(mesh):
    placed = (P(BOTH, None),) + (P("dp", "tensor"),) * 6
    return jax.shard_map(
        local,
        mesh=mesh,
        in_specs=placed,
        out_specs=(P(BOTH, None),) + (P("dp", "tensor"),) * 5 + (P(None, "tensor"), P()),
        check_vma=False,
    )
```

```python
import math

import jax
import jax.numpy as jnp
from jax import lax
from jax.experimental import pallas as pl
from jax.experimental.pallas import tpu as pltpu
from jax.sharding import PartitionSpec as P

FEAT_IN = 6144
SIZES = (2, 4, 2, 4, 4)
BOTH = ("dp", "tensor")
NEAR = [list(range(8)), list(range(8, 16))]
BF16, F32 = jnp.bfloat16, jnp.float32


def shift(array, z=0, y=0, core=0, x=0, high=0):
    moves = (z, y, core, x, high)
    pairs = []
    for source in range(math.prod(SIZES)):
        rest, place = source, []
        for size in reversed(SIZES):
            place.append(rest % size)
            rest //= size
        target = 0
        for size, at, move in zip(SIZES, reversed(place), moves):
            target = target * size + (at + move) % size
        pairs.append((source, target))
    return lax.ppermute(array, BOTH, pairs)


def roll(array, start):
    return lax.dynamic_slice_in_dim(
        jnp.concatenate([array, array], axis=0), start, array.shape[0], axis=0
    )


def take(array, index, axis):
    return lax.dynamic_index_in_dim(array, index, axis, keepdims=False)


def after(array, *others):
    return lax.optimization_barrier((array,) + others)[0]


def total_of(row, axis):
    spread = jnp.broadcast_to(row[None], (16, 8, 128))
    return jnp.sum(lax.all_to_all(spread, axis, 0, 0, tiled=True), axis=0)


def moments_kernel(
    own, other, master, mcode, mscale, scode, sscale,
    update, new_mcode, new_mscale, new_scode, new_sscale, sums,
):
    rows, cols = master.shape
    blocks = mscale.shape[1]
    wide = cols // blocks
    step = 64
    sums[...] = jnp.zeros_like(sums)

    def body(i, carry):
        at = pl.ds(pl.multiple_of(i * step, step), step)
        mscales, sscales = mscale[at, :], sscale[at, :]
        new_m, new_s = [], []
        for b in range(blocks):
            cut = slice(b * wide, (b + 1) * wide)
            grad = own[at, cut] + other[at, cut].astype(F32)
            weight = master[at, cut]
            moment = mcode[at, cut].astype(F32) * mscales[:, b : b + 1]
            second = scode[at, cut].astype(F32) * sscales[:, b : b + 1]
            moment = 0.9 * moment + 0.1 * grad
            second = 0.999 * second + 0.001 * grad * grad
            change = (
                moment / (1.0 - 0.9**10) / (jnp.sqrt(second / (1.0 - 0.999**10)) + 1e-06)
                + 0.1 * weight
            )
            update[at, cut] = change
            mtop = 2.0 * jnp.max(jnp.abs(moment), axis=1, keepdims=True) + 1e-06
            stop = 2.0 * jnp.max(jnp.abs(second), axis=1, keepdims=True) + 1e-06
            new_mcode[at, cut] = (moment / mtop).astype(BF16)
            new_scode[at, cut] = (second / stop).astype(BF16)
            new_m.append(mtop)
            new_s.append(stop)
            sums[0:1, :] += jnp.sum(weight * weight, axis=0, keepdims=True)
            sums[1:2, :] += jnp.sum(change * change, axis=0, keepdims=True)
        new_mscale[at, :] = jnp.concatenate(new_m, axis=1)
        new_sscale[at, :] = jnp.concatenate(new_s, axis=1)
        return carry

    lax.fori_loop(0, rows // step, body, 0)
    sums[...] = jnp.broadcast_to(jnp.sum(sums[...], axis=1, keepdims=True), sums.shape)


def moments(own, other, master, mcode, mscale, scode, sscale):
    like = lambda a, dtype: jax.ShapeDtypeStruct(a.shape, dtype)
    block = master.shape[1] // mscale.shape[1]
    return pl.pallas_call(
        moments_kernel,
        out_shape=(
            like(master, F32),
            like(master, BF16),
            like(mscale, F32),
            like(master, BF16),
            like(sscale, F32),
            jax.ShapeDtypeStruct((8, block), F32),
        ),
        in_specs=[pl.BlockSpec(memory_space=pltpu.VMEM)] * 7,
        out_specs=[pl.BlockSpec(memory_space=pltpu.VMEM)] * 6,
        compiler_params=pltpu.CompilerParams(vmem_limit_bytes=32 * 1024 * 1024),
        cost_estimate=pl.CostEstimate(
            flops=master.size, bytes_accessed=master.size, transcendentals=0
        ),
    )(own, other, master, mcode, mscale, scode, sscale)


def local(layer_input, out_grad, master, moment_code, moment_scale, second_code, second_scale):
    inv_root = 1.0 / math.sqrt(FEAT_IN)
    d, t = lax.axis_index("dp"), lax.axis_index("tensor")
    z, x, high = d // 8, t // 4, t % 4
    few, feat = layer_input.shape
    rows, cols = master.shape
    steps = (1, 2, 3)

    grads = out_grad.reshape(4, 4, few, cols).transpose(1, 0, 2, 3)
    grads = roll(grads[::-1], 3 - high)
    parts = [take(grads, x, 1)] + [shift(take(grads, (x + s) % 4, 1), x=s) for s in steps]
    mine = layer_input.reshape(few, 2, 8, rows).transpose(2, 0, 1, 3).reshape(8, few, 2 * rows)
    mine = lax.all_to_all(mine, "dp", 0, 0, tiled=True, axis_index_groups=NEAR)
    moved = [shift(mine, high=s) for s in steps]
    weights = master.astype(BF16)
    far = shift(weights, z=1)
    parts, far = lax.optimization_barrier((parts, mine, far))[::2]
    weights = jnp.concatenate([jnp.where(z == 0, weights, far), jnp.where(z == 0, far, weights)])
    weights = jnp.concatenate([weights] + [shift(weights, x=s) for s in steps], axis=1)
    near = jnp.concatenate(parts, axis=2).reshape(4 * few, 4 * cols)
    wide = lax.all_gather(near, "dp", axis=0, tiled=True, axis_index_groups=NEAR)

    acts = jnp.stack([mine] + moved, axis=1).reshape(32 * few, 2 * rows)

    acts = after(acts, weights)
    part = jnp.einsum("tk,tn->kn", acts, wide, preferred_element_type=F32) * inv_root
    part = [part[:, s * cols : (s + 1) * cols] for s in range(4)]
    sends = [part[s].astype(BF16) for s in steps]
    others = [shift(send, x=-s) for s, send in zip(steps, sends)]

    weights = after(weights, *sends)
    outs = jnp.einsum("tn,kn->tk", wide, weights, preferred_element_type=F32) * inv_root
    outs = outs.reshape(8, 4, few, 2 * rows)
    pieces = [outs[:, s].astype(BF16) for s in steps]
    others = lax.optimization_barrier((tuple(others), tuple(pieces)))[0]
    grad = part[0] + sum(other.astype(F32) for other in others)
    grad = grad.reshape(2, rows, cols)
    far = shift(take(grad, 1 - z, 0).astype(BF16), z=1)
    update, new_moment_code, new_moment_scale, new_second_code, new_second_scale, sums = moments(
        take(grad, z, 0), far, master, moment_code, moment_scale, second_code, second_scale
    )
    summed = outs[:, 0]
    for s, piece in zip(steps, pieces):
        summed = summed + shift(piece, high=-s).astype(F32)
    sums = total_of(sums, "dp")
    summed, sums = lax.optimization_barrier((summed, sums))
    sums = total_of(sums, "tensor")
    weight_sq, update_sq = sums[0, 0], sums[1, 0]
    trust_ratio = jnp.sqrt(weight_sq) / (jnp.sqrt(update_sq) + 1e-06)
    rate = 0.02 * trust_ratio
    new_master = master - rate * update
    new_weight = lax.all_gather(new_master.astype(BF16), "dp", axis=0, tiled=True)

    back = lax.all_to_all(
        after(summed.astype(BF16), sums), "dp", 0, 0, tiled=True, axis_index_groups=NEAR
    )
    input_grad = back.reshape(8, few, 2, rows).transpose(1, 2, 0, 3).reshape(few, feat)

    return (
        input_grad,
        new_master,
        new_moment_code,
        new_moment_scale,
        new_second_code,
        new_second_scale,
        new_weight,
        trust_ratio,
    )


def solution(mesh):
    placed = (P(BOTH, None),) + (P("dp", "tensor"),) * 6
    return jax.shard_map(
        local,
        mesh=mesh,
        in_specs=placed,
        out_specs=(P(BOTH, None),) + (P("dp", "tensor"),) * 5 + (P(None, "tensor"), P()),
        check_vma=False,
    )
```

```python
import math

import jax
import jax.numpy as jnp
from jax import lax
from jax.experimental import pallas as pl
from jax.experimental.pallas import tpu as pltpu
from jax.sharding import PartitionSpec as P

FEAT_IN = 6144
SIZES = (2, 4, 2, 4, 4)
BOTH = ("dp", "tensor")
NEAR = [list(range(8)), list(range(8, 16))]
LINE = [[4 * x + high for high in range(4)] for x in range(4)]
BF16, F32 = jnp.bfloat16, jnp.float32


def shift(array, z=0, y=0, core=0, x=0, high=0):
    moves = (z, y, core, x, high)
    pairs = []
    for source in range(math.prod(SIZES)):
        rest, place = source, []
        for size in reversed(SIZES):
            place.append(rest % size)
            rest //= size
        target = 0
        for size, at, move in zip(SIZES, reversed(place), moves):
            target = target * size + (at + move) % size
        pairs.append((source, target))
    return lax.ppermute(array, BOTH, pairs)


def take(array, index, axis):
    return lax.dynamic_index_in_dim(array, index, axis, keepdims=False)


def after(array, *others):
    return lax.optimization_barrier((array,) + others)[0]


def total_of(row, axis):
    spread = jnp.broadcast_to(row[None], (16, 8, 128))
    return jnp.sum(lax.all_to_all(spread, axis, 0, 0, tiled=True), axis=0)


def moments_kernel(
    upper, far, lower, one, two, three, master, mcode, mscale, scode, sscale,
    update, new_mcode, new_mscale, new_scode, new_sscale, sums,
):
    rows, cols = master.shape
    blocks = mscale.shape[1]
    wide = cols // blocks
    step = 64
    steps = rows // 2 // step
    sums[...] = jnp.zeros_like(sums)

    def some(i, gradient):
        at = pl.ds(pl.multiple_of(i * step, step), step)
        mscales, sscales = mscale[at, :], sscale[at, :]
        new_m, new_s = [], []
        for b in range(blocks):
            cut = slice(b * wide, (b + 1) * wide)
            grad = gradient(cut)
            weight = master[at, cut]
            moment = mcode[at, cut].astype(F32) * mscales[:, b : b + 1]
            second = scode[at, cut].astype(F32) * sscales[:, b : b + 1]
            moment = 0.9 * moment + 0.1 * grad
            second = 0.999 * second + 0.001 * grad * grad
            change = (
                moment / (1.0 - 0.9**10) / (jnp.sqrt(second / (1.0 - 0.999**10)) + 1e-06)
                + 0.1 * weight
            )
            update[at, cut] = change
            mtop = 2.0 * jnp.max(jnp.abs(moment), axis=1, keepdims=True) + 1e-06
            stop = 2.0 * jnp.max(jnp.abs(second), axis=1, keepdims=True) + 1e-06
            new_mcode[at, cut] = (moment / mtop).astype(BF16)
            new_scode[at, cut] = (second / stop).astype(BF16)
            new_m.append(mtop)
            new_s.append(stop)
            sums[0:1, :] += jnp.sum(weight * weight, axis=0, keepdims=True)
            sums[1:2, :] += jnp.sum(change * change, axis=0, keepdims=True)
        new_mscale[at, :] = jnp.concatenate(new_m, axis=1)
        new_sscale[at, :] = jnp.concatenate(new_s, axis=1)

    def body(i, carry):
        at = pl.ds(pl.multiple_of(i * step, step), step)
        some(i, lambda cut: upper[at, cut] + far[at, cut].astype(F32))
        some(
            i + steps,
            lambda cut: lower[at, cut]
            + one[at, cut].astype(F32)
            + two[at, cut].astype(F32)
            + three[at, cut].astype(F32),
        )
        return carry

    lax.fori_loop(0, steps, body, 0)
    sums[...] = jnp.broadcast_to(jnp.sum(sums[...], axis=1, keepdims=True), sums.shape)


def moments(upper, far, lower, others, master, mcode, mscale, scode, sscale):
    like = lambda a, dtype: jax.ShapeDtypeStruct(a.shape, dtype)
    block = master.shape[1] // mscale.shape[1]
    return pl.pallas_call(
        moments_kernel,
        out_shape=(
            like(master, F32),
            like(master, BF16),
            like(mscale, F32),
            like(master, BF16),
            like(sscale, F32),
            jax.ShapeDtypeStruct((8, block), F32),
        ),
        in_specs=[pl.BlockSpec(memory_space=pltpu.VMEM)] * 11,
        out_specs=[pl.BlockSpec(memory_space=pltpu.VMEM)] * 6,
        compiler_params=pltpu.CompilerParams(vmem_limit_bytes=32 * 1024 * 1024),
        cost_estimate=pl.CostEstimate(
            flops=master.size, bytes_accessed=master.size, transcendentals=0
        ),
    )(upper, far, lower, *others, master, mcode, mscale, scode, sscale)


def local(layer_input, out_grad, master, moment_code, moment_scale, second_code, second_scale):
    inv_root = 1.0 / math.sqrt(FEAT_IN)
    d, t = lax.axis_index("dp"), lax.axis_index("tensor")
    z, x, high = d // 8, t // 4, t % 4
    few, feat = layer_input.shape
    rows, cols = master.shape
    steps = (1, 2, 3)

    grads = out_grad.reshape(4, 4, few, cols)
    parts = [take(grads, x, 0)] + [shift(take(grads, (x + s) % 4, 0), x=s) for s in steps]
    mine = layer_input.reshape(few, 2, 8, rows).transpose(2, 0, 1, 3).reshape(8, few, 2 * rows)
    mine = lax.all_to_all(mine, "dp", 0, 0, tiled=True, axis_index_groups=NEAR)
    weights = master.astype(BF16)
    far = shift(weights, z=1)
    parts, far = lax.optimization_barrier((parts, mine, far))[::2]
    weights = jnp.concatenate([jnp.where(z == 0, weights, far), jnp.where(z == 0, far, weights)])
    moved = [shift(mine, high=1), shift(mine, high=-1)]
    wings = [shift(weights, x=1), shift(weights, x=-1)]
    moved, wings = lax.optimization_barrier((moved, wings))
    across = [shift(moved[0][:4], high=1), shift(moved[1][4:], high=-1)]
    moved = [moved[0], jnp.concatenate(across), moved[1]]
    across = [shift(wings[0][:rows], x=1), shift(wings[1][rows:], x=-1)]
    near = jnp.concatenate(parts, axis=2).reshape(4 * few, 4 * cols)
    wide = lax.all_gather(near, "dp", axis=0, tiled=True, axis_index_groups=NEAR)

    groups = wide.reshape(8, 4, few, 4 * cols)
    part = sum(
        jnp.einsum(
            "tk,tn->kn",
            piece.reshape(8 * few, 2 * rows),
            take(groups, (high + 4 - q) % 4, 1).reshape(8 * few, 4 * cols),
            preferred_element_type=F32,
        )
        for q, piece in enumerate([mine] + moved)
    )
    part = (part * inv_root).reshape(2, rows, 4 * cols)
    half = rows // 2
    block = lambda a, s: a[..., s * cols : (s + 1) * cols]
    upper, lower = part[:, :half], part[:, half:]
    sends = [block(upper, s).astype(BF16) for s in steps]
    sends.append(take(lower, 1 - z, 0).astype(BF16))
    others = [shift(send, x=-s) for s, send in zip(steps, sends)]
    others, crossed = lax.optimization_barrier((others, shift(sends[3], z=1)))
    lower = take(lower, z, 0) + crossed.astype(F32)
    upper = block(upper, 0) + sum(other.astype(F32) for other in others)
    far = shift(take(upper, 1 - z, 0).astype(BF16), z=1)
    others = [shift(block(lower, s).astype(BF16), x=-s) for s in steps]

    across = lax.optimization_barrier((across, sends))[0]
    weights = jnp.concatenate([weights, wings[0], jnp.concatenate(across), wings[1]], axis=1)
    outs = jnp.einsum("tn,kn->tk", wide, weights, preferred_element_type=F32) * inv_root
    outs = after(outs.astype(BF16), lower).reshape(8, 4, few, 2 * rows).transpose(1, 0, 2, 3)
    summed = lax.psum_scatter(
        outs.reshape(32 * few, 2 * rows), "tensor", scatter_dimension=0, tiled=True, axis_index_groups=LINE
    ).reshape(8, few, 2 * rows)

    update, new_moment_code, new_moment_scale, new_second_code, new_second_scale, sums = moments(
        take(upper, z, 0), far, block(lower, 0), others,
        master, moment_code, moment_scale, second_code, second_scale,
    )
    sums = total_of(sums, "dp")
    summed, sums = lax.optimization_barrier((summed, sums))
    sums = total_of(sums, "tensor")
    weight_sq, update_sq = sums[0, 0], sums[1, 0]
    trust_ratio = jnp.sqrt(weight_sq) / (jnp.sqrt(update_sq) + 1e-06)
    rate = 0.02 * trust_ratio
    new_master = master - rate * update
    new_weight = lax.all_gather(new_master.astype(BF16), "dp", axis=0, tiled=True)

    back = lax.all_to_all(
        after(summed, sums), "dp", 0, 0, tiled=True, axis_index_groups=NEAR
    )
    input_grad = back.reshape(8, few, 2, rows).transpose(1, 2, 0, 3).reshape(few, feat)

    return (
        input_grad,
        new_master,
        new_moment_code,
        new_moment_scale,
        new_second_code,
        new_second_scale,
        new_weight,
        trust_ratio,
    )


def solution(mesh):
    placed = (P(BOTH, None),) + (P("dp", "tensor"),) * 6
    return jax.shard_map(
        local,
        mesh=mesh,
        in_specs=placed,
        out_specs=(P(BOTH, None),) + (P("dp", "tensor"),) * 5 + (P(None, "tensor"), P()),
        check_vma=False,
    )
```

```python
import math

import jax
import jax.numpy as jnp
from jax import lax
from jax.experimental import pallas as pl
from jax.experimental.pallas import tpu as pltpu
from jax.sharding import PartitionSpec as P

FEAT_IN = 6144
SIZES = (2, 4, 2, 4, 4)
BOTH = ("dp", "tensor")
NEAR = [list(range(8)), list(range(8, 16))]
LINE = [[4 * x + high for high in range(4)] for x in range(4)]
BF16, F32 = jnp.bfloat16, jnp.float32


def shift(array, z=0, y=0, core=0, x=0, high=0):
    moves = (z, y, core, x, high)
    pairs = []
    for source in range(math.prod(SIZES)):
        rest, place = source, []
        for size in reversed(SIZES):
            place.append(rest % size)
            rest //= size
        target = 0
        for size, at, move in zip(SIZES, reversed(place), moves):
            target = target * size + (at + move) % size
        pairs.append((source, target))
    return lax.ppermute(array, BOTH, pairs)


def take(array, index, axis):
    return lax.dynamic_index_in_dim(array, index, axis, keepdims=False)


def after(array, *others):
    return lax.optimization_barrier((array,) + others)[0]


def moments_kernel(
    upper, far, lower, one, two, three, master, mcode, mscale, scode, sscale,
    update, new_mcode, new_mscale, new_scode, new_sscale, spread, sums,
):
    rows, cols = master.shape
    blocks = mscale.shape[1]
    wide = cols // blocks
    step = 64
    steps = rows // 2 // step
    sums[...] = jnp.zeros_like(sums)

    def some(i, gradient):
        at = pl.ds(pl.multiple_of(i * step, step), step)
        mscales, sscales = mscale[at, :], sscale[at, :]
        new_m, new_s = [], []
        for b in range(blocks):
            cut = slice(b * wide, (b + 1) * wide)
            grad = gradient(cut)
            weight = master[at, cut]
            moment = mcode[at, cut].astype(F32) * mscales[:, b : b + 1]
            second = scode[at, cut].astype(F32) * sscales[:, b : b + 1]
            moment = 0.9 * moment + 0.1 * grad
            second = 0.999 * second + 0.001 * grad * grad
            change = (
                moment / (1.0 - 0.9**10) / (jnp.sqrt(second / (1.0 - 0.999**10)) + 1e-06)
                + 0.1 * weight
            )
            update[at, cut] = change
            mtop = 2.0 * jnp.max(jnp.abs(moment), axis=1, keepdims=True) + 1e-06
            stop = 2.0 * jnp.max(jnp.abs(second), axis=1, keepdims=True) + 1e-06
            new_mcode[at, cut] = (moment / mtop).astype(BF16)
            new_scode[at, cut] = (second / stop).astype(BF16)
            new_m.append(mtop)
            new_s.append(stop)
            sums[0:1, :] += jnp.sum(weight * weight, axis=0, keepdims=True)
            sums[1:2, :] += jnp.sum(change * change, axis=0, keepdims=True)
        new_mscale[at, :] = jnp.concatenate(new_m, axis=1)
        new_sscale[at, :] = jnp.concatenate(new_s, axis=1)

    def body(i, carry):
        at = pl.ds(pl.multiple_of(i * step, step), step)
        some(i, lambda cut: upper[at, cut] + far[at, cut].astype(F32))
        some(
            i + steps,
            lambda cut: lower[at, cut]
            + one[at, cut].astype(F32)
            + two[at, cut].astype(F32)
            + three[at, cut].astype(F32),
        )
        return carry

    lax.fori_loop(0, steps, body, 0)
    totals = jnp.broadcast_to(jnp.sum(sums[...], axis=1, keepdims=True), sums.shape)
    for i in range(spread.shape[0]):
        spread[i] = totals


def moments(upper, far, lower, others, master, mcode, mscale, scode, sscale):
    like = lambda a, dtype: jax.ShapeDtypeStruct(a.shape, dtype)
    return pl.pallas_call(
        moments_kernel,
        out_shape=(
            like(master, F32),
            like(master, BF16),
            like(mscale, F32),
            like(master, BF16),
            like(sscale, F32),
            jax.ShapeDtypeStruct((16, 8, 128), F32),
        ),
        in_specs=[pl.BlockSpec(memory_space=pltpu.VMEM)] * 11,
        out_specs=[pl.BlockSpec(memory_space=pltpu.VMEM)] * 6,
        scratch_shapes=[pltpu.VMEM((8, 128), F32)],
        compiler_params=pltpu.CompilerParams(vmem_limit_bytes=32 * 1024 * 1024),
        cost_estimate=pl.CostEstimate(
            flops=master.size, bytes_accessed=master.size, transcendentals=0
        ),
    )(upper, far, lower, *others, master, mcode, mscale, scode, sscale)


def finish_kernel(sums, master, update, new_master, new16, trust):
    row = jnp.sum(sums[...], axis=0)
    ratio = jnp.sqrt(row[0:1, :]) / (jnp.sqrt(row[1:2, :]) + 1e-06)
    trust[...] = jnp.broadcast_to(ratio, trust.shape)
    rate = 0.02 * ratio
    rows, cols = master.shape
    for at in range(0, cols, 128):
        cut = slice(at, at + 128)
        fresh = master[:, cut] - rate * update[:, cut]
        new_master[:, cut] = fresh
        new16[:, cut] = fresh.astype(BF16)


def finish(sums, master, update):
    whole = pl.BlockSpec(memory_space=pltpu.VMEM)
    return pl.pallas_call(
        finish_kernel,
        out_shape=(
            jax.ShapeDtypeStruct(master.shape, F32),
            jax.ShapeDtypeStruct(master.shape, BF16),
            jax.ShapeDtypeStruct((8, 128), F32),
        ),
        in_specs=[whole] * 3,
        out_specs=[whole] * 3,
        compiler_params=pltpu.CompilerParams(vmem_limit_bytes=32 * 1024 * 1024),
        cost_estimate=pl.CostEstimate(
            flops=master.size, bytes_accessed=master.size, transcendentals=0
        ),
    )(sums, master, update)


def local(layer_input, out_grad, master, moment_code, moment_scale, second_code, second_scale):
    inv_root = 1.0 / math.sqrt(FEAT_IN)
    d, t = lax.axis_index("dp"), lax.axis_index("tensor")
    z, x, high = d // 8, t // 4, t % 4
    few, feat = layer_input.shape
    rows, cols = master.shape
    steps = (1, 2, 3)

    grads = out_grad.reshape(4, 4, few, cols)
    parts = [take(grads, x, 0)] + [shift(take(grads, (x + s) % 4, 0), x=s) for s in steps]
    mine = layer_input.reshape(few, 2, 8, rows).transpose(2, 0, 1, 3).reshape(8, few, 2 * rows)
    mine = lax.all_to_all(mine, "dp", 0, 0, tiled=True, axis_index_groups=NEAR)
    weights = master.astype(BF16)
    far = shift(weights, z=1)
    parts, far = lax.optimization_barrier((parts, mine, far))[::2]
    weights = jnp.concatenate([jnp.where(z == 0, weights, far), jnp.where(z == 0, far, weights)])
    moved = [shift(mine, high=1), shift(mine, high=-1)]
    wings = [shift(weights, x=1), shift(weights, x=-1)]
    moved, wings = lax.optimization_barrier((moved, wings))
    across = [shift(moved[0][:4], high=1), shift(moved[1][4:], high=-1)]
    pieces = [(mine, 0, 0), (moved[0], 1, 0), (moved[1], 3, 0), (across[0], 2, 0), (across[1], 2, 4)]
    across = [shift(wings[0][:rows], x=1), shift(wings[1][rows:], x=-1)]
    near = jnp.concatenate(parts, axis=2).reshape(4 * few, 4 * cols)
    wide = lax.all_gather(near, "dp", axis=0, tiled=True, axis_index_groups=NEAR)

    groups = wide.reshape(8, 4, few, 4 * cols)
    cuts = [
        take(groups, (high + 4 - q) % 4, 1)[at : at + len(piece)].reshape(-1, 4 * cols)
        for piece, q, at in pieces
    ]
    ready, cuts = lax.optimization_barrier(([piece for piece, _, _ in pieces], cuts))
    part = sum(
        jnp.einsum(
            "tk,tn->kn", piece.reshape(-1, 2 * rows), cut, preferred_element_type=F32
        )
        for piece, cut in zip(ready, cuts)
    )
    part = (part * inv_root).reshape(2, rows, 4 * cols)
    half = rows // 2
    block = lambda a, s: a[..., s * cols : (s + 1) * cols]
    upper, lower = part[:, :half], part[:, half:]
    sends = [block(upper, s).astype(BF16) for s in steps]
    sends.append(take(lower, 1 - z, 0).astype(BF16))
    others = [shift(send, x=-s) for s, send in zip(steps, sends)]
    others, crossed = lax.optimization_barrier((others, shift(sends[3], z=1)))
    lower = take(lower, z, 0) + crossed.astype(F32)
    upper = block(upper, 0) + sum(other.astype(F32) for other in others)
    far = shift(take(upper, 1 - z, 0).astype(BF16), z=1)
    others = [shift(block(lower, s).astype(BF16), x=-s) for s in steps]

    across = lax.optimization_barrier((across, sends))[0]
    weights = jnp.concatenate([weights, wings[0], jnp.concatenate(across), wings[1]], axis=1)
    outs = jnp.einsum("tn,kn->tk", wide, weights, preferred_element_type=F32) * inv_root
    outs = after(outs.astype(BF16), lower).reshape(8, 4, few, 2 * rows).transpose(1, 0, 2, 3)
    summed = lax.psum_scatter(
        outs.reshape(32 * few, 2 * rows), "tensor", scatter_dimension=0, tiled=True, axis_index_groups=LINE
    ).reshape(8, few, 2 * rows)

    update, new_moment_code, new_moment_scale, new_second_code, new_second_scale, sums = moments(
        take(upper, z, 0), far, block(lower, 0), others,
        master, moment_code, moment_scale, second_code, second_scale,
    )
    spread = jnp.broadcast_to(jnp.sum(lax.all_to_all(sums, "dp", 0, 0, tiled=True), axis=0), sums.shape)
    sums = lax.all_to_all(spread, "tensor", 0, 0, tiled=True)
    new_master, new16, trust_ratio = finish(sums, master, update)
    new_weight = lax.all_gather(after(new16, summed), "dp", axis=0, tiled=True)
    trust_ratio = trust_ratio[0, 0]

    back = lax.all_to_all(
        after(summed, sums), "dp", 0, 0, tiled=True, axis_index_groups=NEAR
    )
    input_grad = back.reshape(8, few, 2, rows).transpose(1, 2, 0, 3).reshape(few, feat)

    return (
        input_grad,
        new_master,
        new_moment_code,
        new_moment_scale,
        new_second_code,
        new_second_scale,
        new_weight,
        trust_ratio,
    )


def solution(mesh):
    placed = (P(BOTH, None),) + (P("dp", "tensor"),) * 6
    return jax.shard_map(
        local,
        mesh=mesh,
        in_specs=placed,
        out_specs=(P(BOTH, None),) + (P("dp", "tensor"),) * 5 + (P(None, "tensor"), P()),
        check_vma=False,
    )
```

```python
import math

import jax
import jax.numpy as jnp
from jax import lax
from jax.experimental import pallas as pl
from jax.experimental.pallas import tpu as pltpu
from jax.sharding import PartitionSpec as P

FEAT_IN = 6144
SIZES = (2, 4, 2, 4, 4)
BOTH = ("dp", "tensor")
NEAR = [list(range(8)), list(range(8, 16))]
LINE = [[4 * x + high for high in range(4)] for x in range(4)]
BF16, F32 = jnp.bfloat16, jnp.float32


def shift(array, z=0, y=0, core=0, x=0, high=0):
    moves = (z, y, core, x, high)
    pairs = []
    for source in range(math.prod(SIZES)):
        rest, place = source, []
        for size in reversed(SIZES):
            place.append(rest % size)
            rest //= size
        target = 0
        for size, at, move in zip(SIZES, reversed(place), moves):
            target = target * size + (at + move) % size
        pairs.append((source, target))
    return lax.ppermute(array, BOTH, pairs)


def take(array, index, axis):
    return lax.dynamic_index_in_dim(array, index, axis, keepdims=False)


def after(array, *others):
    return lax.optimization_barrier((array,) + others)[0]


def moments_kernel(
    upper, far, lower, one, two, three, master, mcode, mscale, scode, sscale,
    update, new_mcode, new_mscale, new_scode, new_sscale, spread, sums,
):
    rows, cols = master.shape
    blocks = mscale.shape[1]
    wide = cols // blocks
    step = 64
    steps = rows // 2 // step
    sums[...] = jnp.zeros_like(sums)

    def some(i, gradient):
        at = pl.ds(pl.multiple_of(i * step, step), step)
        mscales, sscales = mscale[at, :], sscale[at, :]
        new_m, new_s = [], []
        for b in range(blocks):
            cut = slice(b * wide, (b + 1) * wide)
            grad = gradient(cut)
            weight = master[at, cut]
            moment = mcode[at, cut].astype(F32) * mscales[:, b : b + 1]
            second = scode[at, cut].astype(F32) * sscales[:, b : b + 1]
            moment = 0.9 * moment + 0.1 * grad
            second = 0.999 * second + 0.001 * grad * grad
            change = (
                moment / (1.0 - 0.9**10) / (jnp.sqrt(second / (1.0 - 0.999**10)) + 1e-06)
                + 0.1 * weight
            )
            update[at, cut] = change
            mtop = 2.0 * jnp.max(jnp.abs(moment), axis=1, keepdims=True) + 1e-06
            stop = 2.0 * jnp.max(jnp.abs(second), axis=1, keepdims=True) + 1e-06
            new_mcode[at, cut] = (moment / mtop).astype(BF16)
            new_scode[at, cut] = (second / stop).astype(BF16)
            new_m.append(mtop)
            new_s.append(stop)
            sums[0:1, :] += jnp.sum(weight * weight, axis=0, keepdims=True)
            sums[1:2, :] += jnp.sum(change * change, axis=0, keepdims=True)
        new_mscale[at, :] = jnp.concatenate(new_m, axis=1)
        new_sscale[at, :] = jnp.concatenate(new_s, axis=1)

    def body(i, carry):
        at = pl.ds(pl.multiple_of(i * step, step), step)
        some(i, lambda cut: upper[at, cut] + far[at, cut].astype(F32))
        some(
            i + steps,
            lambda cut: lower[at, cut]
            + one[at, cut].astype(F32)
            + two[at, cut].astype(F32)
            + three[at, cut].astype(F32),
        )
        return carry

    lax.fori_loop(0, steps, body, 0)
    totals = jnp.broadcast_to(jnp.sum(sums[...], axis=1, keepdims=True), sums.shape)
    for i in range(spread.shape[0]):
        spread[i] = totals


def moments(upper, far, lower, others, master, mcode, mscale, scode, sscale):
    like = lambda a, dtype: jax.ShapeDtypeStruct(a.shape, dtype)
    return pl.pallas_call(
        moments_kernel,
        out_shape=(
            like(master, F32),
            like(master, BF16),
            like(mscale, F32),
            like(master, BF16),
            like(sscale, F32),
            jax.ShapeDtypeStruct((16, 8, 128), F32),
        ),
        in_specs=[pl.BlockSpec(memory_space=pltpu.VMEM)] * 11,
        out_specs=[pl.BlockSpec(memory_space=pltpu.VMEM)] * 6,
        scratch_shapes=[pltpu.VMEM((8, 128), F32)],
        compiler_params=pltpu.CompilerParams(vmem_limit_bytes=32 * 1024 * 1024),
        cost_estimate=pl.CostEstimate(
            flops=master.size, bytes_accessed=master.size, transcendentals=0
        ),
    )(upper, far, lower, *others, master, mcode, mscale, scode, sscale)


def finish_kernel(sums, master, update, new_master, new16, trust):
    row = jnp.sum(sums[...], axis=0)
    ratio = jnp.sqrt(row[0:1, :]) / (jnp.sqrt(row[1:2, :]) + 1e-06)
    trust[...] = jnp.broadcast_to(ratio, trust.shape)
    rate = 0.02 * ratio
    rows, cols = master.shape
    for at in range(0, cols, 128):
        cut = slice(at, at + 128)
        fresh = master[:, cut] - rate * update[:, cut]
        new_master[:, cut] = fresh
        new16[:, cut] = fresh.astype(BF16)


def finish(sums, master, update):
    whole = pl.BlockSpec(memory_space=pltpu.VMEM)
    return pl.pallas_call(
        finish_kernel,
        out_shape=(
            jax.ShapeDtypeStruct(master.shape, F32),
            jax.ShapeDtypeStruct(master.shape, BF16),
            jax.ShapeDtypeStruct((8, 128), F32),
        ),
        in_specs=[whole] * 3,
        out_specs=[whole] * 3,
        compiler_params=pltpu.CompilerParams(vmem_limit_bytes=32 * 1024 * 1024),
        cost_estimate=pl.CostEstimate(
            flops=master.size, bytes_accessed=master.size, transcendentals=0
        ),
    )(sums, master, update)


def copy_kernel(source, target):
    target[...] = source[...]


def copied(array):
    rows, cols = array.shape
    some = pl.BlockSpec((rows // 6, cols), lambda i: (i, 0))
    return pl.pallas_call(
        copy_kernel,
        out_shape=jax.ShapeDtypeStruct(array.shape, array.dtype),
        grid=(6,),
        in_specs=[some],
        out_specs=some,
        compiler_params=pltpu.CompilerParams(vmem_limit_bytes=16 * 1024 * 1024),
        cost_estimate=pl.CostEstimate(flops=0, bytes_accessed=4 * array.size, transcendentals=0),
    )(array)


def local(layer_input, out_grad, master, moment_code, moment_scale, second_code, second_scale):
    inv_root = 1.0 / math.sqrt(FEAT_IN)
    d, t = lax.axis_index("dp"), lax.axis_index("tensor")
    z, x, high = d // 8, t // 4, t % 4
    few, feat = layer_input.shape
    rows, cols = master.shape
    steps = (1, 2, 3)

    grads = out_grad.reshape(4, 4, few, cols)
    parts = [take(grads, x, 0)] + [shift(take(grads, (x + s) % 4, 0), x=s) for s in steps]
    mine = layer_input.reshape(few, 2, 8, rows).transpose(2, 0, 1, 3).reshape(8, few, 2 * rows)
    mine = lax.all_to_all(mine, "dp", 0, 0, tiled=True, axis_index_groups=NEAR)
    weights = master.astype(BF16)
    far = shift(weights, z=1)
    parts, far = lax.optimization_barrier((parts, mine, far))[::2]
    weights = jnp.concatenate([jnp.where(z == 0, weights, far), jnp.where(z == 0, far, weights)])
    moved = [shift(mine, high=1), shift(mine, high=-1)]
    wings = [shift(weights, x=1), shift(weights, x=-1)]
    moved, wings = lax.optimization_barrier((moved, wings))
    across = [shift(moved[0][:4], high=1), shift(moved[1][4:], high=-1)]
    pieces = [(mine, 0, 0), (moved[0], 1, 0), (moved[1], 3, 0), (across[0], 2, 0), (across[1], 2, 4)]
    across = [shift(wings[0][:rows], x=1), shift(wings[1][rows:], x=-1)]
    near = jnp.concatenate(parts, axis=2).reshape(4 * few, 4 * cols)
    wide = lax.all_gather(near, "dp", axis=0, tiled=True, axis_index_groups=NEAR)

    groups = wide.reshape(8, 4, few, 4 * cols)
    cuts = [
        take(groups, (high + 4 - q) % 4, 1)[at : at + len(piece)].reshape(-1, 4 * cols)
        for piece, q, at in pieces
    ]
    ready, cuts = lax.optimization_barrier(([piece for piece, _, _ in pieces], cuts))
    part = sum(
        jnp.einsum(
            "tk,tn->kn", piece.reshape(-1, 2 * rows), cut, preferred_element_type=F32
        )
        for piece, cut in zip(ready, cuts)
    )
    part = (part * inv_root).reshape(2, rows, 4 * cols)
    half = rows // 2
    block = lambda a, s: a[..., s * cols : (s + 1) * cols]
    upper, lower = part[:, :half], part[:, half:]
    sends = [block(upper, s).astype(BF16) for s in steps]
    sends.append(take(lower, 1 - z, 0).astype(BF16))
    others = [shift(send, x=-s) for s, send in zip(steps, sends)]
    others, crossed = lax.optimization_barrier((others, shift(sends[3], z=1)))
    lower = take(lower, z, 0) + crossed.astype(F32)
    upper = block(upper, 0) + sum(other.astype(F32) for other in others)
    far = shift(take(upper, 1 - z, 0).astype(BF16), z=1)
    others = [shift(block(lower, s).astype(BF16), x=-s) for s in steps]

    across = lax.optimization_barrier((across, sends))[0]
    weights = jnp.concatenate([weights, wings[0], jnp.concatenate(across), wings[1]], axis=1)
    outs = jnp.einsum("tn,kn->tk", wide, weights, preferred_element_type=F32) * inv_root
    outs = outs.astype(BF16).reshape(8, 4, few, 2 * rows).transpose(1, 0, 2, 3)
    outs = after(outs.reshape(32 * few, 2 * rows), lower)
    summed = lax.psum_scatter(
        outs, "tensor", scatter_dimension=0, tiled=True, axis_index_groups=LINE
    ).reshape(8, few, 2 * rows)

    update, new_moment_code, new_moment_scale, new_second_code, new_second_scale, sums = moments(
        take(upper, z, 0), far, block(lower, 0), others,
        master, moment_code, moment_scale, second_code, second_scale,
    )
    spread = jnp.broadcast_to(jnp.sum(lax.all_to_all(sums, "dp", 0, 0, tiled=True), axis=0), sums.shape)
    sums = lax.all_to_all(spread, "tensor", 0, 0, tiled=True)
    new_master, new16, trust_ratio = finish(sums, master, update)
    new_weight = lax.all_gather(after(new16, summed), "dp", axis=0, tiled=True)
    new_weight = copied(new_weight)
    trust_ratio = trust_ratio[0, 0]

    back = lax.all_to_all(
        after(summed, sums), "dp", 0, 0, tiled=True, axis_index_groups=NEAR
    )
    input_grad = back.reshape(8, few, 2, rows).transpose(1, 2, 0, 3).reshape(few, feat)

    return (
        input_grad,
        new_master,
        new_moment_code,
        new_moment_scale,
        new_second_code,
        new_second_scale,
        new_weight,
        trust_ratio,
    )


def solution(mesh):
    placed = (P(BOTH, None),) + (P("dp", "tensor"),) * 6
    return jax.shard_map(
        local,
        mesh=mesh,
        in_specs=placed,
        out_specs=(P(BOTH, None),) + (P("dp", "tensor"),) * 5 + (P(None, "tensor"), P()),
        check_vma=False,
    )
```

```python
import math

import jax
import jax.numpy as jnp
from jax import lax
from jax.experimental import pallas as pl
from jax.experimental.pallas import tpu as pltpu
from jax.sharding import PartitionSpec as P

FEAT_IN = 6144
SIZES = (2, 4, 2, 4, 4)
BOTH = ("dp", "tensor")
NEAR = [list(range(8)), list(range(8, 16))]
LINE = [[4 * x + high for high in range(4)] for x in range(4)]
BF16, F32 = jnp.bfloat16, jnp.float32


def shift(array, z=0, y=0, core=0, x=0, high=0):
    moves = (z, y, core, x, high)
    pairs = []
    for source in range(math.prod(SIZES)):
        rest, place = source, []
        for size in reversed(SIZES):
            place.append(rest % size)
            rest //= size
        target = 0
        for size, at, move in zip(SIZES, reversed(place), moves):
            target = target * size + (at + move) % size
        pairs.append((source, target))
    return lax.ppermute(array, BOTH, pairs)


def take(array, index, axis):
    return lax.dynamic_index_in_dim(array, index, axis, keepdims=False)


def after(array, *others):
    return lax.optimization_barrier((array,) + others)[0]


def moments_kernel(
    upper, far, lower, one, two, three, master, mcode, mscale, scode, sscale,
    update, new_mcode, new_mscale, new_scode, new_sscale, spread, sums,
):
    rows, cols = master.shape
    blocks = mscale.shape[1]
    wide = cols // blocks
    step = 64
    steps = rows // 2 // step
    sums[...] = jnp.zeros_like(sums)

    def some(i, gradient):
        at = pl.ds(pl.multiple_of(i * step, step), step)
        mscales, sscales = mscale[at, :], sscale[at, :]
        new_m, new_s = [], []
        for b in range(blocks):
            cut = slice(b * wide, (b + 1) * wide)
            grad = gradient(cut)
            weight = master[at, cut]
            moment = mcode[at, cut].astype(F32) * mscales[:, b : b + 1]
            second = scode[at, cut].astype(F32) * sscales[:, b : b + 1]
            moment = 0.9 * moment + 0.1 * grad
            second = 0.999 * second + 0.001 * grad * grad
            change = (
                moment / (1.0 - 0.9**10) / (jnp.sqrt(second / (1.0 - 0.999**10)) + 1e-06)
                + 0.1 * weight
            )
            update[at, cut] = change
            mtop = 2.0 * jnp.max(jnp.abs(moment), axis=1, keepdims=True) + 1e-06
            stop = 2.0 * jnp.max(jnp.abs(second), axis=1, keepdims=True) + 1e-06
            new_mcode[at, cut] = (moment / mtop).astype(BF16)
            new_scode[at, cut] = (second / stop).astype(BF16)
            new_m.append(mtop)
            new_s.append(stop)
            sums[0:1, :] += jnp.sum(weight * weight, axis=0, keepdims=True)
            sums[1:2, :] += jnp.sum(change * change, axis=0, keepdims=True)
        new_mscale[at, :] = jnp.concatenate(new_m, axis=1)
        new_sscale[at, :] = jnp.concatenate(new_s, axis=1)

    def body(i, carry):
        at = pl.ds(pl.multiple_of(i * step, step), step)
        some(i, lambda cut: upper[at, cut] + far[at, cut].astype(F32))
        some(
            i + steps,
            lambda cut: lower[at, cut]
            + one[at, cut].astype(F32)
            + two[at, cut].astype(F32)
            + three[at, cut].astype(F32),
        )
        return carry

    lax.fori_loop(0, steps, body, 0)
    totals = jnp.broadcast_to(jnp.sum(sums[...], axis=1, keepdims=True), sums.shape)
    for i in range(spread.shape[0]):
        spread[i] = totals


def moments(upper, far, lower, others, master, mcode, mscale, scode, sscale):
    like = lambda a, dtype: jax.ShapeDtypeStruct(a.shape, dtype)
    return pl.pallas_call(
        moments_kernel,
        out_shape=(
            like(master, F32),
            like(master, BF16),
            like(mscale, F32),
            like(master, BF16),
            like(sscale, F32),
            jax.ShapeDtypeStruct((16, 8, 128), F32),
        ),
        in_specs=[pl.BlockSpec(memory_space=pltpu.VMEM)] * 11,
        out_specs=[pl.BlockSpec(memory_space=pltpu.VMEM)] * 6,
        scratch_shapes=[pltpu.VMEM((8, 128), F32)],
        compiler_params=pltpu.CompilerParams(vmem_limit_bytes=32 * 1024 * 1024),
        cost_estimate=pl.CostEstimate(
            flops=master.size, bytes_accessed=master.size, transcendentals=0
        ),
    )(upper, far, lower, *others, master, mcode, mscale, scode, sscale)


def finish_kernel(sums, master, update, new_master, new16, trust):
    row = jnp.sum(sums[...], axis=0)
    ratio = jnp.sqrt(row[0:1, :]) / (jnp.sqrt(row[1:2, :]) + 1e-06)
    trust[...] = jnp.broadcast_to(ratio, trust.shape)
    rate = 0.02 * ratio
    rows, cols = master.shape
    for at in range(0, cols, 128):
        cut = slice(at, at + 128)
        fresh = master[:, cut] - rate * update[:, cut]
        new_master[:, cut] = fresh
        new16[:, cut] = fresh.astype(BF16)


def finish(sums, master, update):
    whole = pl.BlockSpec(memory_space=pltpu.VMEM)
    return pl.pallas_call(
        finish_kernel,
        out_shape=(
            jax.ShapeDtypeStruct(master.shape, F32),
            jax.ShapeDtypeStruct(master.shape, BF16),
            jax.ShapeDtypeStruct((8, 128), F32),
        ),
        in_specs=[whole] * 3,
        out_specs=[whole] * 3,
        compiler_params=pltpu.CompilerParams(vmem_limit_bytes=32 * 1024 * 1024),
        cost_estimate=pl.CostEstimate(
            flops=master.size, bytes_accessed=master.size, transcendentals=0
        ),
    )(sums, master, update)


def copy_kernel(source, target):
    target[...] = source[...]


def copied(array):
    rows, cols = array.shape
    some = pl.BlockSpec((rows // 6, cols), lambda i: (i, 0))
    return pl.pallas_call(
        copy_kernel,
        out_shape=jax.ShapeDtypeStruct(array.shape, array.dtype),
        grid=(6,),
        in_specs=[some],
        out_specs=some,
        compiler_params=pltpu.CompilerParams(vmem_limit_bytes=60 * 1024 * 1024),
        cost_estimate=pl.CostEstimate(flops=0, bytes_accessed=4 * array.size, transcendentals=0),
    )(array)


def local(layer_input, out_grad, master, moment_code, moment_scale, second_code, second_scale):
    inv_root = 1.0 / math.sqrt(FEAT_IN)
    d, t = lax.axis_index("dp"), lax.axis_index("tensor")
    z, x, high = d // 8, t // 4, t % 4
    few, feat = layer_input.shape
    rows, cols = master.shape
    steps = (1, 2, 3)

    grads = out_grad.reshape(4, 4, few, cols)
    parts = [take(grads, x, 0)] + [shift(take(grads, (x + s) % 4, 0), x=s) for s in steps]
    mine = layer_input.reshape(few, 2, 8, rows).transpose(2, 0, 1, 3).reshape(8, few, 2 * rows)
    mine = lax.all_to_all(mine, "dp", 0, 0, tiled=True, axis_index_groups=NEAR)
    weights = master.astype(BF16)
    far = shift(weights, z=1)
    parts, far = lax.optimization_barrier((parts, mine, far))[::2]
    weights = jnp.concatenate([jnp.where(z == 0, weights, far), jnp.where(z == 0, far, weights)])
    moved = [shift(mine, high=1), shift(mine, high=-1)]
    wings = [shift(weights, x=1), shift(weights, x=-1)]
    moved, wings = lax.optimization_barrier((moved, wings))
    across = [shift(moved[0][:4], high=1), shift(moved[1][4:], high=-1)]
    pieces = [(mine, 0, 0), (moved[0], 1, 0), (moved[1], 3, 0), (across[0], 2, 0), (across[1], 2, 4)]
    across = [shift(wings[0][:rows], x=1), shift(wings[1][rows:], x=-1)]
    near = jnp.concatenate(parts, axis=2).reshape(4 * few, 4 * cols)
    wide = lax.all_gather(near, "dp", axis=0, tiled=True, axis_index_groups=NEAR)

    groups = wide.reshape(8, 4, few, 4 * cols)
    cuts = [
        take(groups, (high + 4 - q) % 4, 1)[at : at + len(piece)].reshape(-1, 4 * cols)
        for piece, q, at in pieces
    ]
    ready, cuts = lax.optimization_barrier(([piece for piece, _, _ in pieces], cuts))
    part = sum(
        jnp.einsum(
            "tk,tn->kn", piece.reshape(-1, 2 * rows), cut, preferred_element_type=F32
        )
        for piece, cut in zip(ready, cuts)
    )
    part = (part * inv_root).reshape(2, rows, 4 * cols)
    half = rows // 2
    block = lambda a, s: a[..., s * cols : (s + 1) * cols]
    upper, lower = part[:, :half], part[:, half:]
    sends = [block(upper, s).astype(BF16) for s in steps]
    sends.append(take(lower, 1 - z, 0).astype(BF16))
    others = [shift(send, x=-s) for s, send in zip(steps, sends)]
    others, crossed = lax.optimization_barrier((others, shift(sends[3], z=1)))
    lower = take(lower, z, 0) + crossed.astype(F32)
    upper = block(upper, 0) + sum(other.astype(F32) for other in others)
    far = shift(take(upper, 1 - z, 0).astype(BF16), z=1)
    others = [shift(block(lower, s).astype(BF16), x=-s) for s in steps]

    across = lax.optimization_barrier((across, sends))[0]
    weights = jnp.concatenate([weights, wings[0], jnp.concatenate(across), wings[1]], axis=1)
    outs = jnp.einsum("tn,kn->tk", wide, weights, preferred_element_type=F32) * inv_root
    outs = outs.astype(BF16).reshape(8, 4, few, 2 * rows).transpose(1, 0, 2, 3)
    outs = after(outs.reshape(32 * few, 2 * rows), lower)
    summed = lax.psum_scatter(
        outs, "tensor", scatter_dimension=0, tiled=True, axis_index_groups=LINE
    ).reshape(8, few, 2 * rows)

    update, new_moment_code, new_moment_scale, new_second_code, new_second_scale, sums = moments(
        take(upper, z, 0), far, block(lower, 0), others,
        master, moment_code, moment_scale, second_code, second_scale,
    )
    spread = jnp.broadcast_to(jnp.sum(lax.all_to_all(sums, "dp", 0, 0, tiled=True), axis=0), sums.shape)
    sums = lax.all_to_all(spread, "tensor", 0, 0, tiled=True)
    new_master, new16, trust_ratio = finish(sums, master, update)
    new_weight = lax.all_gather(after(new16, summed), "dp", axis=0, tiled=True)
    new_weight = copied(new_weight)
    trust_ratio = trust_ratio[0, 0]

    back = lax.all_to_all(
        after(summed, sums), "dp", 0, 0, tiled=True, axis_index_groups=NEAR
    )
    input_grad = back.reshape(8, few, 2, rows).transpose(1, 2, 0, 3).reshape(few, feat)

    return (
        input_grad,
        new_master,
        new_moment_code,
        new_moment_scale,
        new_second_code,
        new_second_scale,
        new_weight,
        trust_ratio,
    )


def solution(mesh):
    placed = (P(BOTH, None),) + (P("dp", "tensor"),) * 6
    return jax.shard_map(
        local,
        mesh=mesh,
        in_specs=placed,
        out_specs=(P(BOTH, None),) + (P("dp", "tensor"),) * 5 + (P(None, "tensor"), P()),
        check_vma=False,
    )
```
